256 devices in a mesh: half: 2 (over y_lo), row: 8 (over z), col: 16 (over y_hi, x, core).
Axes of the slice: x: 4, y: 4 (y_hi: 2, y_lo: 2; y = y_hi * 2 + y_lo), z: 8, core: 2. Of those that a mesh axis runs over, the one named last changes fastest.
Arguments:
- front: float32 [16384, 16384], P('row', ('col', 'half')), may hold values from -6 to 6
- children: float32 [2, 8192, 8192], P('half', 'row', 'col'), may hold values from -6 to 6
- child_map: int32 [2, 64], replicated, may hold values from 0 to 127, as said below
- inverses: float32 [2, 512, 512], replicated, as said below
Outputs:
- factored: float32 [16384, 16384], P('row', ('col', 'half'))
The draws below stay inside these ranges and needn't reach their ends.
Inputs may be any that keep to these rules, and one draw needn't show every extreme that they name: child_map[c, k] is 2 k or 2 k + 1: each child covers one tile of every pair of parent tiles. `inverses`: upper triangular, entries on and above the diagonal independent.
All inputs are finite; a program needn't handle non-finite values.
Results may differ from the reference program's by a relative error of at most 0.0001.
Values sent between devices are 32-bit elements; how exact they have to be, the bound alone decides.
A program may use at most 128 MiB of HBM per device.

```python
import jax
import jax.numpy as jnp
from jax import lax

NF = 16384
NC = 8192
TILE = 128
NCT = 64
PW = 512
PANELS = 2


def draw_child_map(key, part):
    key = jax.random.fold_in(key, 11)
    bits = jax.random.randint(key, (2, NCT), 0, 2, dtype=jnp.int32)
    return 2 * jnp.arange(NCT, dtype=jnp.int32)[None, :] + bits


def draw_inverses(key, part):
    key = jax.random.fold_in(key, 23)
    diag_key = jax.random.fold_in(key, 5)
    base = 0.54 * float(PW) ** (-0.25)
    spread = 0.3 * base * float(PW) ** (-0.5)
    values = jnp.clip(jax.random.normal(key, (PANELS, PW, PW), jnp.float32), -4.0, 4.0) * spread
    diagonal = jax.random.uniform(diag_key, (PANELS, PW), jnp.float32, 0.8, 1.2) * base
    identity = jnp.eye(PW, dtype=jnp.float32)
    upper = jnp.triu(values, 1)
    return (upper + diagonal[:, :, None] * identity[None, :, :]).astype(jnp.float32)


def shard_levels(rng, dims, shards, low, largest):
    def one(dim, shards_of):
        steps = jax.random.uniform(jax.random.fold_in(jax.random.fold_in(rng, 6), dim), (shards_of,), jnp.float32, low / len(shards), largest / len(shards))
        return jnp.repeat(jnp.exp(steps), dims[dim] // shards_of).reshape((-1,) + (1,) * (len(dims) - dim - 1))

    loudness = one(*shards[0])
    for cut in shards[1:]:
        loudness = loudness * one(*cut)
    return loudness


def gaussian(key, dims, deviation, most, cuts=(), kind=jnp.bfloat16):
    level = shard_levels(key, dims, cuts, -0.22, 0.18) if cuts else 1.0
    drawn = jax.random.normal(key, dims, jnp.float32) * deviation * level
    return jnp.minimum(jnp.maximum(drawn, -most), most).astype(kind)


def setup_inputs(seed: int = 0) -> dict:
    arg_keys = jax.random.split(jax.random.key(seed), 5)
    return {
        "front": gaussian(arg_keys[0], (NF, NF), 1.0, 6.0, ((0, 8), (1, 32)), jnp.float32),
        "children": gaussian(arg_keys[1], (2, NC, NC), 1.0, 6.0, ((0, 2), (1, 8), (2, 16)), jnp.float32),
        "child_map": draw_child_map(jax.random.fold_in(arg_keys[4], 71), 0),
        "inverses": draw_inverses(jax.random.fold_in(arg_keys[4], 71), 0),
    }


def reference(front, children, child_map, inverses):
    offsets = jnp.arange(TILE, dtype=jnp.int32)
    assembled = front
    for child in range(2):
        index = (child_map[child][:, None] * TILE + offsets[None, :]).reshape(NC).astype(jnp.int32)
        spread = jnp.zeros((NF, NC), jnp.float32).at[index].add(children[child])
        assembled = assembled.at[:, index].add(spread)
    positions = jnp.arange(NF, dtype=jnp.int32)
    for panel in range(PANELS):
        first = panel * PW
        slab = assembled[:, first:first + PW]
        factor = jnp.dot(slab, inverses[panel], precision=lax.Precision.HIGHEST, preferred_element_type=jnp.float32)
        keep = (positions >= first + PW)[:, None]
        factor = jnp.where(keep, factor, jnp.zeros_like(factor))
        assembled = assembled - jnp.dot(factor, factor.T, precision=lax.Precision.HIGHEST, preferred_element_type=jnp.float32)
        columns = assembled[:, first:first + PW]
        assembled = assembled.at[:, first:first + PW].set(jnp.where(keep, factor, columns))
    return assembled
```

```python
import jax
import jax.numpy as jnp
from jax import lax
from jax.experimental import pallas as pl
from jax.experimental.pallas import tpu as pltpu
from jax.sharding import PartitionSpec as P

TILE = 128
PW = 512
ROWS = 2048
COLS = 512
CHILD_ROWS = 1024
HALF_COLS = 256
TILES = ROWS // TILE
ITEM = 32
TREES = 4
NZ = 8
RING_CHUNKS = 8
STEPS = 28
F32 = jnp.float32
BF16 = jnp.bfloat16


def split(value):
    high = value.astype(BF16)
    return high, (value - high.astype(F32)).astype(BF16)


def dot(left, right):
    return lax.dot_general(left, right, (((1,), (0,)), ((), ())), preferred_element_type=F32)


def dot3(left, right):
    (lh, ll), (rh, rl) = left, right
    return dot(lh, rh) + (dot(lh, rl) + dot(ll, rh))


def tile_of(chunk):
    return 8 * (chunk // 8) + (chunk // 2) % 4 + 4 * (1 - chunk % 2)


def kernel(
    map_ref,
    front_hbm,
    child_hbm,
    inv_hbm,
    out_hbm,
    front,
    own,
    got,
    inv,
    inv_hi,
    inv_lo,
    rows,
    cross,
    wide,
    y_hi,
    y_lo,
    out,
    load_sem,
    store_sem,
    child_send,
    child_recv,
    tree_send,
    tree_recv,
    feed_send,
    mate_send,
    mate_recv,
    ring_send,
    ring_recv,
    cross_send,
    cross_recv,
    wide_send,
    wide_recv,
    widemate_send,
    widemate_recv,
):
    half = lax.axis_index("half")
    z = lax.axis_index("row")
    col = lax.axis_index("col")
    core = col % 2
    x = (col // 2) % 4
    yh = col // 8
    y = 2 * yh + half
    block = 2 * col + half

    mate = {"col": col + 1 - 2 * core}
    other = {"half": 1 - half}
    near_x = {"col": col + 2 * (1 - 2 * (x % 2))}
    far_x = {"col": col + 2 * (3 - 2 * x)}
    far_y = {"half": 1 - half, "col": col + 8 * (1 - 2 * yh)}
    links = (other, near_x, far_y, far_x)
    up = {"row": (z + 1) % NZ}
    down = {"row": (z + NZ - 1) % NZ}

    def remote(src, dst, send, recv, device):
        return pltpu.make_async_remote_copy(
            src_ref=src,
            dst_ref=dst,
            send_sem=send,
            recv_sem=recv,
            device_id=device,
            device_id_type=pl.DeviceIdType.MESH,
        )

    def wait_for(ref, sem):
        pltpu.make_async_copy(ref, ref, sem).wait()

    bits = (((y + 1) // 2 + core) % 2, ((x + 1) // 2) % 2, yh, x // 2)
    root = (bits[0] + bits[1] + bits[2] + bits[3]) == 0
    depth = []
    forward = []
    for tree in range(TREES):
        turned = [bits[(tree + 1 + k) % 4] for k in range(4)]
        turned[3] = 1 - turned[3]
        weight = turned[0] + turned[1] + turned[2] + turned[3]
        depth.append(jnp.where(root, 0, 1 + weight))
        flags = [None] * 4
        for k in range(4):
            above = turned[k]
            for later in range(k + 1, 4):
                above = above + turned[later]
            flag = jnp.logical_and(jnp.logical_not(root), above == 0)
            if k == 3:
                flag = jnp.logical_or(root, jnp.logical_and(flag, weight > 0))
            flags[(tree + 1 + k) % 4] = flag
        forward.append(flags)

    owner = jnp.logical_and(jnp.logical_and(x == 0, core == 0), y < 2)
    feeder = jnp.logical_and(owner, half == 1)
    fed = jnp.logical_and(root, core == 1)
    seeded = jnp.logical_and(root, core == 0)

    loads = [
        pltpu.make_async_copy(front_hbm, front, load_sem.at[0]),
        pltpu.make_async_copy(
            child_hbm.at[0, :, pl.ds(pl.multiple_of(half * HALF_COLS, HALF_COLS), HALF_COLS)],
            own,
            load_sem.at[1],
        ),
        pltpu.make_async_copy(inv_hbm, inv, load_sem.at[2]),
    ]
    for load in loads:
        load.start()
    barrier = pltpu.get_barrier_semaphore()
    for device in (mate, up, down) + links:
        pl.semaphore_signal(barrier, inc=1, device_id=device, device_id_type=pl.DeviceIdType.MESH)
    pl.semaphore_wait(barrier, 7)

    def child_piece(piece):
        theirs = pl.ds(pl.multiple_of((1 - half) * HALF_COLS, HALF_COLS), HALF_COLS)
        lines = pl.ds(pl.multiple_of(piece * TILE, TILE), TILE)
        return remote(
            child_hbm.at[0, lines, theirs], got.at[lines], child_send, child_recv.at[piece], other
        )

    @pl.when(owner)
    def _():
        for piece in (2, 0, 3, 1, 6, 4, 7, 5):
            child_piece(piece).start()

    for load in loads:
        load.wait()
    for panel in range(2):
        high, low = split(inv[panel])
        inv_hi[panel] = high
        inv_lo[panel] = low

    def assemble(tile):
        pair = tile // 2
        lines = pl.ds(pl.multiple_of(tile * TILE, TILE), TILE)
        child_lines = pl.ds(pl.multiple_of(pair * TILE, TILE), TILE)
        row_tile = z * (TILES // 2) + pair
        parts = []
        for q in range(4):
            value = front[lines, pl.ds(q * TILE, TILE)]
            col_tile = 4 * col + 2 * half + q // 2
            for ref, which in ((own, half), (got, 1 - half)):
                row_bit = map_ref[which, row_tile] - 2 * row_tile
                col_bit = map_ref[which, col_tile] - 2 * col_tile
                hit = jnp.logical_and(row_bit == tile % 2, col_bit == q % 2)
                value = value + jnp.where(hit, ref[child_lines, pl.ds(q // 2 * TILE, TILE)], 0.0)
            parts.append(value)
        return jnp.concatenate(parts, axis=1)

    def step(t, carry):
        @pl.when(jnp.logical_and(owner, t < TILES))
        def _():
            tile = tile_of(t)

            @pl.when(t % 4 < 2)
            def _():
                piece = tile // 2
                wait_for(got.at[pl.ds(pl.multiple_of(piece * TILE, TILE), TILE)], child_recv.at[piece])

            slab = assemble(tile)
            factor = dot3(split(slab), (inv_hi[half], inv_lo[half]))
            keep = z * TILES + tile >= 4 * (half + 1)
            start = pl.multiple_of(tile * TILE, TILE)
            rows[half, pl.ds(start, TILE)] = jnp.where(keep, factor, 0.0)

            @pl.when(feeder)
            def _():
                for tree in range(TREES):
                    item = rows.at[1, pl.ds(start + ITEM * tree, ITEM)]
                    remote(item, item, feed_send, tree_recv.at[tree, t], mate).start()

        @pl.when(jnp.logical_and(jnp.logical_not(owner), jnp.logical_and(t % 2 == 0, t < 16)))
        def _():
            child_piece(t // 2).start()

        for tree in range(TREES):
            chunk = t - depth[tree]

            @pl.when(jnp.logical_and(chunk >= 0, chunk < TILES))
            def _():
                start = pl.multiple_of(tile_of(chunk) * TILE + ITEM * tree, ITEM)
                item = rows.at[core, pl.ds(start, ITEM)]

                @pl.when(jnp.logical_not(seeded))
                def _():
                    wait_for(item, tree_recv.at[tree, chunk])

                for link in range(4):

                    @pl.when(forward[tree][link])
                    def _():
                        remote(
                            item,
                            item,
                            tree_send.at[tree, link],
                            tree_recv.at[tree, chunk],
                            links[link],
                        ).start()

                @pl.when(jnp.logical_not(fed))
                def _():
                    remote(item, item, mate_send, mate_recv, mate).start()

        for tree in range(TREES):
            onward = up if tree < 2 else down
            hops = (z - 4 * yh - x + 2 * NZ) % NZ if tree < 2 else (4 * yh + x - z + NZ) % NZ
            late = t - (1 - half) - depth[tree] - hops
            chunk = late // 2

            @pl.when(
                jnp.logical_and(late >= 0, jnp.logical_and(late % 2 == 0, chunk < RING_CHUNKS))
            )
            def _():
                which = chunk // 4
                place = pl.multiple_of((chunk % 4) * TILE + ITEM * tree, ITEM)
                item = cross.at[which, pl.ds(place, ITEM)]

                @pl.when(hops == 0)
                def _():
                    tile = 8 * which + 4 * half + chunk % 4
                    start = pl.multiple_of(tile * TILE + ITEM * tree, ITEM)
                    cross[which, pl.ds(place, ITEM)] = rows[core, pl.ds(start, ITEM)]

                @pl.when(hops > 0)
                def _():
                    wait_for(item, ring_recv.at[tree, chunk])

                @pl.when(hops < NZ - 1)
                def _():
                    remote(
                        item, item, ring_send.at[tree], ring_recv.at[tree, chunk], onward
                    ).start()

                @pl.when(which != core)
                def _():
                    remote(
                        item, cross.at[2, pl.ds(place, ITEM)], cross_send, cross_recv, mate
                    ).start()

        for tree in range(TREES):
            onward = up if tree < 2 else down
            hops = z if tree < 2 else (NZ - z) % NZ
            late = t - depth[tree] - hops
            chunk = late // 2

            @pl.when(
                jnp.logical_and(
                    core == 0,
                    jnp.logical_and(late >= 0, jnp.logical_and(late % 2 == 0, chunk < 4)),
                )
            )
            def _():
                place = pl.multiple_of(chunk * TILE + ITEM * tree, ITEM)
                item = wide.at[pl.ds(place, ITEM)]

                @pl.when(hops == 0)
                def _():
                    wide[pl.ds(place, ITEM)] = rows[0, pl.ds(4 * TILE + place, ITEM)]

                @pl.when(hops > 0)
                def _():
                    wait_for(item, wide_recv.at[tree, chunk])

                @pl.when(hops < NZ - 1)
                def _():
                    remote(
                        item, item, wide_send.at[tree], wide_recv.at[tree, chunk], onward
                    ).start()

                remote(item, item, widemate_send, widemate_recv, mate).start()

        return carry

    lax.fori_loop(0, STEPS, step, 0)

    @pl.when(jnp.logical_not(feeder))
    def _():
        wait_for(rows.at[1 - core], mate_recv)

    wait_for(cross.at[2], cross_recv)

    @pl.when(core == 1)
    def _():
        wait_for(wide, widemate_recv)

    @pl.when(jnp.logical_not(owner))
    def _():
        for piece in range(8):
            wait_for(got.at[pl.ds(piece * TILE, TILE)], child_recv.at[piece])

    f0c_t = cross[jnp.where(core == 0, 0, 2)].T
    g1c_t = cross[jnp.where(core == 0, 2, 1)].T
    mixed_t = dot3(split(inv[1].T), split(wide[...]))
    mixed = mixed_t.T
    second = block == 1
    f1c_t = g1c_t - dot3(split(mixed_t), split(f0c_t))
    y0_t = jnp.where(second, mixed, f0c_t - dot3(split(mixed), split(f1c_t)))
    y1_t = jnp.where(second, 0.0, f1c_t)
    for index, value in ((0, y0_t), (1, y1_t), (2, f0c_t)):
        high, low = split(value)
        y_hi[index] = high
        y_lo[index] = low

    def update(tile, carry):
        lines = pl.ds(pl.multiple_of(tile * TILE, TILE), TILE)
        place = z * TILES + tile
        f0 = rows[0, lines]
        g1 = rows[1, lines]
        base = assemble(tile)
        base = jnp.where(jnp.logical_and(block == 0, place >= 4), f0, base)
        base = jnp.where(jnp.logical_and(second, place >= 8), g1, base)
        first = jnp.where(place < 8, 2, 0)
        total = dot3(split(f0), (y_hi[first], y_lo[first]))
        total = total + dot3(split(g1), (y_hi[1], y_lo[1]))
        out[lines] = base - total
        pltpu.make_async_copy(out.at[lines], out_hbm.at[lines], store_sem).start()
        return carry

    lax.fori_loop(0, TILES, update, 0)

    wait_for(out, store_sem)
    wait_for(got, child_send)

    @pl.when(feeder)
    def _():
        wait_for(rows.at[0], feed_send)

    @pl.when(jnp.logical_not(fed))
    def _():
        wait_for(rows.at[0], mate_send)

    wait_for(cross.at[0], cross_send)
    for tree in range(TREES):
        for link in range(4):

            @pl.when(forward[tree][link])
            def _():
                wait_for(rows.at[0, pl.ds(0, TILES * ITEM)], tree_send.at[tree, link])

        hops = (z - 4 * yh - x + 2 * NZ) % NZ if tree < 2 else (4 * yh + x - z + NZ) % NZ

        @pl.when(hops < NZ - 1)
        def _():
            wait_for(rows.at[0, pl.ds(0, RING_CHUNKS * ITEM)], ring_send.at[tree])

        hops = z if tree < 2 else (NZ - z) % NZ

        @pl.when(jnp.logical_and(core == 0, hops < NZ - 1))
        def _():
            wait_for(rows.at[0, pl.ds(0, 4 * ITEM)], wide_send.at[tree])

    @pl.when(core == 0)
    def _():
        wait_for(wide, widemate_send)


def local(front, children, child_map, inverses):
    hbm = pl.BlockSpec(memory_space=pl.ANY)
    dma = pltpu.SemaphoreType.DMA
    return pl.pallas_call(
        kernel,
        out_shape=jax.ShapeDtypeStruct((ROWS, COLS), F32),
        in_specs=[pl.BlockSpec(memory_space=pltpu.SMEM), hbm, hbm, hbm],
        out_specs=hbm,
        scratch_shapes=[
            pltpu.VMEM((ROWS, COLS), F32),
            pltpu.VMEM((CHILD_ROWS, HALF_COLS), F32),
            pltpu.VMEM((CHILD_ROWS, HALF_COLS), F32),
            pltpu.VMEM((2, PW, PW), F32),
            pltpu.VMEM((2, PW, PW), BF16),
            pltpu.VMEM((2, PW, PW), BF16),
            pltpu.VMEM((2, ROWS, PW), F32),
            pltpu.VMEM((3, PW, PW), F32),
            pltpu.VMEM((PW, PW), F32),
            pltpu.VMEM((3, PW, COLS), BF16),
            pltpu.VMEM((3, PW, COLS), BF16),
            pltpu.VMEM((ROWS, COLS), F32),
            dma((3,)),
            dma,
            dma,
            dma((8,)),
            dma((TREES, 4)),
            dma((TREES, TILES)),
            dma,
            dma,
            dma,
            dma((TREES,)),
            dma((TREES, RING_CHUNKS)),
            dma,
            dma,
            dma((TREES,)),
            dma((TREES, 4)),
            dma,
            dma,
        ],
        compiler_params=pltpu.CompilerParams(
            collective_id=0, has_side_effects=True, vmem_limit_bytes=56 * 1024 * 1024
        ),
    )(child_map, front, children, inverses)


def solution(mesh):
    return jax.shard_map(
        local,
        mesh=mesh,
        in_specs=(P("row", ("col", "half")), P("half", "row", "col"), P(), P()),
        out_specs=P("row", ("col", "half")),
        check_vma=False,
    )
```

```python
import jax
import jax.numpy as jnp
from jax import lax
from jax.experimental import pallas as pl
from jax.experimental.pallas import tpu as pltpu
from jax.sharding import PartitionSpec as P

TILE = 128
PW = 512
ROWS = 2048
COLS = 512
CHILD_ROWS = 1024
HALF_COLS = 256
TILES = ROWS // TILE
ITEM = 32
PAIR = 2 * ITEM
TREES = 4
NZ = 8
RING_PIECES = 16
SLACK = 3
CHILD_STEP = 18
CHILD_PIECES = 32
LAST = 5 * SLACK
WIDE_STEP = 9 + 7 * SLACK
STEPS = TILES + 1 + 12 * SLACK
F32 = jnp.float32
BF16 = jnp.bfloat16


def split(value):
    high = value.astype(BF16)
    return high, (value - high.astype(F32)).astype(BF16)


def dot(left, right):
    return lax.dot_general(left, right, (((1,), (0,)), ((), ())), preferred_element_type=F32)


def stacked(value):
    high, low = split(value)
    return jnp.concatenate([high, low, high], axis=0)


def dot3(left, right):
    high, low = split(left)
    return dot(jnp.concatenate([high, high, low], axis=1), right)


def tile_of(chunk):
    pair = lax.div(chunk, 2)
    return 8 * lax.rem(pair, 2) + 4 - 4 * lax.rem(chunk, 2) + lax.div(chunk, 4)


def kernel(
    map_ref,
    front_hbm,
    child_hbm,
    inv_hbm,
    out_hbm,
    front,
    own,
    got,
    inv,
    inv3,
    rows,
    cross,
    wide,
    y3,
    out,
    load_sem,
    store_sem,
    child_send,
    child_recv,
    tree_send,
    tree_recv,
    feed_send,
    mate_send,
    mate_recv,
    ring_send,
    ring_recv,
    cross_send,
    cross_recv,
    climb_send,
    climb_recv,
    wide_send,
    wide_recv,
    widemate_send,
    widemate_recv,
):
    half = lax.axis_index("half")
    z = lax.axis_index("row")
    col = lax.axis_index("col")
    core = col % 2
    x = (col // 2) % 4
    yh = col // 8
    y = 2 * yh + half
    block = 2 * col + half

    mate = {"col": col + 1 - 2 * core}
    other = {"half": 1 - half}
    near_x = {"col": col + 2 * (1 - 2 * (x % 2))}
    far_x = {"col": col + 2 * (3 - 2 * x)}
    far_y = {"half": 1 - half, "col": col + 8 * (1 - 2 * yh)}
    links = (other, near_x, far_y, far_x)
    up = {"row": (z + 1) % NZ}
    down = {"row": (z + NZ - 1) % NZ}

    def remote(src, dst, send, recv, peer):
        return pltpu.make_async_remote_copy(
            src_ref=src,
            dst_ref=dst,
            send_sem=send,
            recv_sem=recv,
            device_id=peer,
            device_id_type=pl.DeviceIdType.MESH,
        )

    def wait_for(ref, sem):
        pltpu.make_async_copy(ref, ref, sem).wait()

    bits = (((y + 1) // 2 + core) % 2, ((x + 1) // 2) % 2, yh, x // 2)
    root = (bits[0] + bits[1] + bits[2] + bits[3]) == 0
    depth = []
    forward = []
    for tree in range(TREES):
        turned = [bits[(tree + 1 + k) % 4] for k in range(4)]
        turned[3] = 1 - turned[3]
        weight = turned[0] + turned[1] + turned[2] + turned[3]
        depth.append(jnp.where(root, 0, SLACK * (1 + weight)))
        flags = [None] * 4 + [jnp.logical_or(root, turned[3] == 0)]
        for k in range(4):
            above = turned[k]
            for later in range(k + 1, 4):
                above = above + turned[later]
            flag = jnp.logical_and(jnp.logical_not(root), above == 0)
            if k == 3:
                flag = jnp.logical_or(root, jnp.logical_and(flag, weight > 0))
            flags[(tree + 1 + k) % 4] = flag
        forward.append(flags)

    owner = jnp.logical_and(jnp.logical_and(x == 0, core == 0), y < 2)
    feeder = jnp.logical_and(owner, half == 1)
    fed = jnp.logical_and(root, core == 1)
    seeded = jnp.logical_and(root, core == 0)

    source = 4 * yh + x
    ring_hops = [(z - source + NZ) % NZ, (source - z + NZ) % NZ]
    wide_hops = [z, (NZ - z) % NZ]
    ring_start = [
        1 - half + jnp.maximum(depth[2 * way], depth[2 * way + 1]) + SLACK * ring_hops[way]
        for way in range(2)
    ]

    loads = [
        pltpu.make_async_copy(front_hbm, front, load_sem.at[0]),
        pltpu.make_async_copy(
            child_hbm.at[0, :, pl.ds(pl.multiple_of(half * HALF_COLS, HALF_COLS), HALF_COLS)],
            own,
            load_sem.at[1],
        ),
        pltpu.make_async_copy(inv_hbm, inv, load_sem.at[2]),
    ]
    for load in loads:
        load.start()
    barrier = pltpu.get_barrier_semaphore()
    for peer in (mate, up, down) + links:
        pl.semaphore_signal(barrier, inc=1, device_id=peer, device_id_type=pl.DeviceIdType.MESH)
    pl.semaphore_wait(barrier, 7)

    def child_piece(piece, count, recv):
        theirs = pl.ds(pl.multiple_of((1 - half) * HALF_COLS, HALF_COLS), HALF_COLS)
        lines = pl.ds(pl.multiple_of(piece * count, count), count)
        return remote(
            child_hbm.at[0, lines, theirs], got.at[lines], child_send, recv, other
        )

    @pl.when(owner)
    def _():
        for piece in (2, 0, 6, 4, 3, 1, 7, 5):
            child_piece(piece, TILE, child_recv.at[piece]).start()

    for load in loads:
        load.wait()
    for panel in range(2):
        inv3[panel] = stacked(inv[panel])

    def assemble(tile):
        pair = lax.div(tile, 2)
        lines = pl.ds(pl.multiple_of(tile * TILE, TILE), TILE)
        child_lines = pl.ds(pl.multiple_of(pair * TILE, TILE), TILE)
        row_tile = z * (TILES // 2) + pair
        parts = []
        for q in range(4):
            value = front[lines, pl.ds(q * TILE, TILE)]
            col_tile = 4 * col + 2 * half + q // 2
            for ref, which in ((own, half), (got, 1 - half)):
                row_bit = map_ref[which, row_tile] - 2 * row_tile
                col_bit = map_ref[which, col_tile] - 2 * col_tile
                hit = jnp.logical_and(row_bit == lax.rem(tile, 2), col_bit == q % 2)
                value = value + jnp.where(hit, ref[child_lines, pl.ds(q // 2 * TILE, TILE)], 0.0)
            parts.append(value)
        return jnp.concatenate(parts, axis=1)

    def spread(item, tree, send, recv):
        def give(link):
            @pl.when(forward[tree][link])
            def _():
                remote(item, item, send.at[tree, link], recv, links[link]).start()

        @pl.when(forward[tree][4])
        def _():
            give(tree)
            give((tree + 3) % 4)

            @pl.when(forward[tree][(tree + 2) % 4])
            def _():
                give((tree + 2) % 4)
                give((tree + 1) % 4)

    def step(t, carry):
        @pl.when(jnp.logical_and(owner, t < TILES))
        def _():
            tile = tile_of(t)

            @pl.when(lax.rem(t, 8) < 4)
            def _():
                piece = lax.div(tile, 2)
                wait_for(got.at[pl.ds(pl.multiple_of(piece * TILE, TILE), TILE)], child_recv.at[piece])

            slab = assemble(tile)
            factor = dot3(slab, inv3[half])
            keep = z * TILES + tile >= 4 * (half + 1)
            start = pl.multiple_of(tile * TILE, TILE)
            rows[half, pl.ds(start, TILE)] = jnp.where(keep, factor, 0.0)

            @pl.when(feeder)
            def _():
                for tree in range(TREES):
                    item = rows.at[1, pl.ds(start + ITEM * tree, ITEM)]
                    remote(item, item, feed_send, tree_recv.at[tree, t], mate).start()

        @pl.when(
            jnp.logical_and(
                jnp.logical_not(owner),
                jnp.logical_and(t >= CHILD_STEP, t < CHILD_STEP + CHILD_PIECES),
            )
        )
        def _():
            child_piece(t - CHILD_STEP, CHILD_ROWS // CHILD_PIECES, child_recv.at[0]).start()

        @pl.when(t < TILES + LAST)
        def _():
            for tree in range(TREES):
                chunk = t - depth[tree]

                @pl.when(jnp.logical_and(chunk >= 0, chunk < TILES))
                def _():
                    start = pl.multiple_of(tile_of(chunk) * TILE + ITEM * tree, ITEM)
                    item = rows.at[core, pl.ds(start, ITEM)]

                    @pl.when(jnp.logical_not(seeded))
                    def _():
                        wait_for(item, tree_recv.at[tree, chunk])

                    spread(item, tree, tree_send, tree_recv.at[tree, chunk])

            late = t - LAST

            @pl.when(jnp.logical_and(late >= 0, jnp.logical_not(fed)))
            def _():
                start = pl.multiple_of(tile_of(late) * TILE, TILE)
                item = rows.at[core, pl.ds(start, TILE)]
                remote(item, item, mate_send, mate_recv, mate).start()

        for way in range(2):
            onward = (up, down)[way]
            hops = ring_hops[way]
            piece = t - ring_start[way]

            @pl.when(jnp.logical_and(piece >= 0, piece < RING_PIECES))
            def _():
                which = lax.rem(lax.div(piece, 2), 2)
                place = lax.div(piece, 4) * TILE + PAIR * way + ITEM * lax.rem(piece, 2)
                place = pl.multiple_of(place, ITEM)
                item = cross.at[which, pl.ds(place, ITEM)]

                @pl.when(hops == 0)
                def _():
                    start = pl.multiple_of((8 * which + 4 * half) * TILE + place, ITEM)
                    cross[which, pl.ds(place, ITEM)] = rows[core, pl.ds(start, ITEM)]

                @pl.when(hops > 0)
                def _():
                    wait_for(item, ring_recv.at[way, piece])

                @pl.when(hops < NZ - 1)
                def _():
                    remote(
                        item, item, ring_send.at[way], ring_recv.at[way, piece], onward
                    ).start()

                @pl.when(which != core)
                def _():
                    remote(
                        item, cross.at[2, pl.ds(place, ITEM)], cross_send, cross_recv, mate
                    ).start()

        @pl.when(seeded)
        def _():
            for way in range(2):
                onward = (up, down)[way]
                hops = wide_hops[way]
                late = t - SLACK * hops
                chunk = lax.div(late, 4)

                @pl.when(jnp.logical_and(late >= 0, jnp.logical_and(lax.rem(late, 4) == 0, chunk < 4)))
                def _():
                    place = pl.multiple_of(chunk * TILE + PAIR * way, PAIR)
                    item = wide.at[pl.ds(place, PAIR)]

                    @pl.when(hops == 0)
                    def _():
                        wide[pl.ds(place, PAIR)] = rows[0, pl.ds(4 * TILE + place, PAIR)]

                    @pl.when(hops > 0)
                    def _():
                        wait_for(item, climb_recv.at[way, chunk])

                    @pl.when(hops < NZ - 1)
                    def _():
                        remote(
                            item, item, climb_send.at[way], climb_recv.at[way, chunk], onward
                        ).start()

        @pl.when(jnp.logical_and(core == 0, t >= WIDE_STEP))
        def _():
            for tree in range(TREES):
                part = t - WIDE_STEP - depth[tree]

                @pl.when(jnp.logical_and(part >= 0, part < 4))
                def _():
                    place = pl.multiple_of(part * TILE + ITEM * tree, ITEM)
                    item = wide.at[pl.ds(place, ITEM)]

                    @pl.when(jnp.logical_not(seeded))
                    def _():
                        wait_for(item, wide_recv.at[tree, part])

                    spread(item, tree, wide_send, wide_recv.at[tree, part])

            late = t - WIDE_STEP - LAST

            @pl.when(jnp.logical_and(late >= 0, late < 4))
            def _():
                item = wide.at[pl.ds(pl.multiple_of(late * TILE, TILE), TILE)]
                remote(item, item, widemate_send, widemate_recv, mate).start()

        return carry

    lax.fori_loop(0, STEPS, step, 0)

    @pl.when(jnp.logical_not(feeder))
    def _():
        wait_for(rows.at[1 - core], mate_recv)

    wait_for(cross.at[2], cross_recv)

    @pl.when(core == 1)
    def _():
        wait_for(wide, widemate_recv)

    @pl.when(jnp.logical_not(owner))
    def _():
        wait_for(got, child_recv.at[0])

    f0c_t = cross[jnp.where(core == 0, 0, 2)].T
    g1c_t = cross[jnp.where(core == 0, 2, 1)].T
    mixed_t = dot3(inv[1].T, stacked(wide[...]))
    mixed = mixed_t.T
    second = block == 1
    f1c_t = g1c_t - dot3(mixed_t, stacked(f0c_t))
    y0_t = jnp.where(second, mixed, f0c_t - dot3(mixed, stacked(f1c_t)))
    y1_t = jnp.where(second, 0.0, f1c_t)
    for index, value in ((0, y0_t), (1, y1_t), (2, f0c_t)):
        y3[index] = stacked(value)

    def update(tile, carry):
        lines = pl.ds(pl.multiple_of(tile * TILE, TILE), TILE)
        place = z * TILES + tile
        f0 = rows[0, lines]
        g1 = rows[1, lines]
        base = assemble(tile)
        base = jnp.where(jnp.logical_and(block == 0, place >= 4), f0, base)
        base = jnp.where(jnp.logical_and(second, place >= 8), g1, base)
        first = jnp.where(place < 8, 2, 0)
        total = dot3(f0, y3[first])
        total = total + dot3(g1, y3[1])
        out[lines] = base - total
        pltpu.make_async_copy(out.at[lines], out_hbm.at[lines], store_sem).start()
        return carry

    lax.fori_loop(0, TILES, update, 0)

    wait_for(out, store_sem)
    wait_for(got, child_send)

    @pl.when(feeder)
    def _():
        wait_for(rows.at[0], feed_send)

    @pl.when(jnp.logical_not(fed))
    def _():
        wait_for(rows.at[0], mate_send)

    wait_for(cross.at[0], cross_send)
    for tree in range(TREES):
        for link in range(4):

            @pl.when(forward[tree][link])
            def _():
                wait_for(rows.at[0, pl.ds(0, TILES * ITEM)], tree_send.at[tree, link])

                @pl.when(core == 0)
                def _():
                    wait_for(rows.at[0, pl.ds(0, 4 * ITEM)], wide_send.at[tree, link])

    for way in range(2):

        @pl.when(ring_hops[way] < NZ - 1)
        def _():
            wait_for(cross.at[0], ring_send.at[way])

        @pl.when(jnp.logical_and(seeded, wide_hops[way] < NZ - 1))
        def _():
            wait_for(rows.at[0, pl.ds(0, 4 * PAIR)], climb_send.at[way])

    @pl.when(core == 0)
    def _():
        wait_for(wide, widemate_send)


def local(front, children, child_map, inverses):
    hbm = pl.BlockSpec(memory_space=pl.ANY)
    dma = pltpu.SemaphoreType.DMA
    return pl.pallas_call(
        kernel,
        out_shape=jax.ShapeDtypeStruct((ROWS, COLS), F32),
        in_specs=[pl.BlockSpec(memory_space=pltpu.SMEM), hbm, hbm, hbm],
        out_specs=hbm,
        scratch_shapes=[
            pltpu.VMEM((ROWS, COLS), F32),
            pltpu.VMEM((CHILD_ROWS, HALF_COLS), F32),
            pltpu.VMEM((CHILD_ROWS, HALF_COLS), F32),
            pltpu.VMEM((2, PW, PW), F32),
            pltpu.VMEM((2, 3 * PW, PW), BF16),
            pltpu.VMEM((2, ROWS, PW), F32),
            pltpu.VMEM((3, PW, PW), F32),
            pltpu.VMEM((PW, PW), F32),
            pltpu.VMEM((3, 3 * PW, COLS), BF16),
            pltpu.VMEM((ROWS, COLS), F32),
            dma((3,)),
            dma,
            dma,
            dma((8,)),
            dma((TREES, 4)),
            dma((TREES, TILES)),
            dma,
            dma,
            dma,
            dma((2,)),
            dma((2, RING_PIECES)),
            dma,
            dma,
            dma((2,)),
            dma((2, 4)),
            dma((TREES, 4)),
            dma((TREES, 4)),
            dma,
            dma,
        ],
        compiler_params=pltpu.CompilerParams(
            collective_id=0, has_side_effects=True, vmem_limit_bytes=56 * 1024 * 1024
        ),
    )(child_map, front, children, inverses)


def solution(mesh):
    return jax.shard_map(
        local,
        mesh=mesh,
        in_specs=(P("row", ("col", "half")), P("half", "row", "col"), P(), P()),
        out_specs=P("row", ("col", "half")),
        check_vma=False,
    )
```

```python
import jax
import jax.numpy as jnp
from jax import lax
from jax.experimental import pallas as pl
from jax.experimental.pallas import tpu as pltpu
from jax.sharding import PartitionSpec as P

TILE = 128
PW = 512
ROWS = 2048
COLS = 512
CHILD_ROWS = 1024
HALF_COLS = 256
TILES = ROWS // TILE
BIG = 256
ITEM = 32
PAIR = 2 * ITEM
TREES = 4
NZ = 8
RING_PIECES = 20
LONG_PIECES = 12
NEAR_HOPS = (4, 3)
SLACK = 3
CHILD_STEP = 17
CHILD_PIECES = 32
LAST = 5 * SLACK
WIDE_STEP = 3 + 7 * SLACK
STEPS = LAST + LONG_PIECES + 1 + 7 * SLACK
F32 = jnp.float32
BF16 = jnp.bfloat16


def split(value):
    high = value.astype(BF16)
    return high, (value - high.astype(F32)).astype(BF16)


def dot(left, right):
    return lax.dot_general(left, right, (((1,), (0,)), ((), ())), preferred_element_type=F32)


def stacked(value):
    high, low = split(value)
    return jnp.concatenate([high, low, high], axis=0)


def dot3(left, right):
    high, low = split(left)
    return dot(jnp.concatenate([high, high, low], axis=1), right)


def tile_of(chunk):
    return 8 * lax.div(chunk, 8) + 4 - 4 * lax.rem(chunk, 2) + lax.div(lax.rem(chunk, 8), 2)


def kernel(
    map_ref,
    front_hbm,
    child_hbm,
    inv_hbm,
    out_hbm,
    front,
    own,
    got,
    inv,
    inv3,
    rows,
    cross,
    wide,
    y3,
    out,
    load_sem,
    store_sem,
    child_send,
    child_recv,
    tree_send,
    tree_recv,
    feed_send,
    mate_send,
    mate_recv,
    ring_send,
    ring_recv,
    cross_send,
    cross_recv,
    climb_send,
    climb_recv,
    wide_send,
    wide_recv,
    widemate_send,
    widemate_recv,
):
    half = lax.axis_index("half")
    z = lax.axis_index("row")
    col = lax.axis_index("col")
    core = col % 2
    x = (col // 2) % 4
    yh = col // 8
    y = 2 * yh + half
    block = 2 * col + half

    mate = {"col": col + 1 - 2 * core}
    other = {"half": 1 - half}
    near_x = {"col": col + 2 * (1 - 2 * (x % 2))}
    far_x = {"col": col + 2 * (3 - 2 * x)}
    far_y = {"half": 1 - half, "col": col + 8 * (1 - 2 * yh)}
    links = (other, near_x, far_y, far_x)
    up = {"row": (z + 1) % NZ}
    down = {"row": (z + NZ - 1) % NZ}

    def remote(src, dst, send, recv, peer):
        return pltpu.make_async_remote_copy(
            src_ref=src,
            dst_ref=dst,
            send_sem=send,
            recv_sem=recv,
            device_id=peer,
            device_id_type=pl.DeviceIdType.MESH,
        )

    def wait_for(ref, sem):
        pltpu.make_async_copy(ref, ref, sem).wait()

    bits = (((y + 1) // 2 + core) % 2, ((x + 1) // 2) % 2, yh, x // 2)
    root = (bits[0] + bits[1] + bits[2] + bits[3]) == 0
    depth = []
    forward = []
    for tree in range(TREES):
        turned = [bits[(tree + 1 + k) % 4] for k in range(4)]
        turned[3] = 1 - turned[3]
        weight = turned[0] + turned[1] + turned[2] + turned[3]
        depth.append(jnp.where(root, 0, SLACK * (1 + weight)))
        flags = [None] * 4 + [jnp.logical_or(root, turned[3] == 0)]
        for k in range(4):
            above = turned[k]
            for later in range(k + 1, 4):
                above = above + turned[later]
            flag = jnp.logical_and(jnp.logical_not(root), above == 0)
            if k == 3:
                flag = jnp.logical_or(root, jnp.logical_and(flag, weight > 0))
            flags[(tree + 1 + k) % 4] = flag
        forward.append(flags)

    owner = jnp.logical_and(jnp.logical_and(x == 0, core == 0), y < 2)
    feeder = jnp.logical_and(owner, half == 1)
    fed = jnp.logical_and(root, core == 1)
    seeded = jnp.logical_and(root, core == 0)

    source = 4 * yh + x
    ring_hops = [(z - source + NZ) % NZ, (source - z + NZ) % NZ]
    wide_hops = [z, (NZ - z) % NZ]
    deepest = jnp.maximum(jnp.maximum(depth[0], depth[1]), jnp.maximum(depth[2], depth[3]))
    ring_start = [1 - half + deepest + SLACK * hops for hops in ring_hops]

    loads = [
        pltpu.make_async_copy(front_hbm, front, load_sem.at[0]),
        pltpu.make_async_copy(
            child_hbm.at[0, :, pl.ds(pl.multiple_of(half * HALF_COLS, HALF_COLS), HALF_COLS)],
            own,
            load_sem.at[1],
        ),
        pltpu.make_async_copy(inv_hbm, inv, load_sem.at[2]),
    ]
    for load in loads:
        load.start()
    barrier = pltpu.get_barrier_semaphore()
    for peer in (mate, up, down) + links:
        pl.semaphore_signal(barrier, inc=1, device_id=peer, device_id_type=pl.DeviceIdType.MESH)
    pl.semaphore_wait(barrier, 7)

    def child_piece(piece, count, recv):
        theirs = pl.ds(pl.multiple_of((1 - half) * HALF_COLS, HALF_COLS), HALF_COLS)
        lines = pl.ds(pl.multiple_of(piece * count, count), count)
        return remote(
            child_hbm.at[0, lines, theirs], got.at[lines], child_send, recv, other
        )

    @pl.when(owner)
    def _():
        for piece in (2, 0):
            child_piece(piece, TILE, child_recv.at[piece]).start()

    for load in loads:
        load.wait()
    for panel in range(2):
        inv3[panel] = stacked(inv[panel])

    def assemble(tile):
        pair = lax.div(tile, 2)
        lines = pl.ds(pl.multiple_of(tile * TILE, TILE), TILE)
        child_lines = pl.ds(pl.multiple_of(pair * TILE, TILE), TILE)
        row_tile = z * (TILES // 2) + pair
        parts = []
        for q in range(4):
            value = front[lines, pl.ds(q * TILE, TILE)]
            col_tile = 4 * col + 2 * half + q // 2
            for ref, which in ((own, half), (got, 1 - half)):
                row_bit = map_ref[which, row_tile] - 2 * row_tile
                col_bit = map_ref[which, col_tile] - 2 * col_tile
                hit = jnp.logical_and(row_bit == lax.rem(tile, 2), col_bit == q % 2)
                value = value + jnp.where(hit, ref[child_lines, pl.ds(q // 2 * TILE, TILE)], 0.0)
            parts.append(value)
        return jnp.concatenate(parts, axis=1)

    def spread(item, tree, send, recv):
        def give(link):
            @pl.when(forward[tree][link])
            def _():
                remote(item, item, send.at[tree, link], recv, links[link]).start()

        @pl.when(forward[tree][4])
        def _():
            give(tree)
            give((tree + 3) % 4)

            @pl.when(forward[tree][(tree + 2) % 4])
            def _():
                give((tree + 2) % 4)
                give((tree + 1) % 4)

    def step(t, carry):
        @pl.when(jnp.logical_and(owner, t < TILES))
        def _():
            tile = tile_of(t)

            @pl.when(lax.rem(t, 4) < 2)
            def _():
                piece = lax.div(tile, 2)
                wait_for(got.at[pl.ds(pl.multiple_of(piece * TILE, TILE), TILE)], child_recv.at[piece])

            slab = assemble(tile)
            factor = dot3(slab, inv3[half])
            keep = z * TILES + tile >= 4 * (half + 1)
            start = pl.multiple_of(tile * TILE, TILE)
            rows[half, pl.ds(start, TILE)] = jnp.where(keep, factor, 0.0)

            @pl.when(feeder)
            def _():
                for tree in range(TREES):
                    item = rows.at[1, pl.ds(start + ITEM * tree, ITEM)]
                    remote(item, item, feed_send, tree_recv.at[tree, t], mate).start()

        @pl.when(
            jnp.logical_and(
                jnp.logical_not(owner),
                jnp.logical_and(t >= CHILD_STEP, t < CHILD_STEP + CHILD_PIECES),
            )
        )
        def _():
            child_piece(t - CHILD_STEP, CHILD_ROWS // CHILD_PIECES, child_recv.at[0]).start()

        @pl.when(t < TILES + LAST)
        def _():
            for tree in range(TREES):
                chunk = t - depth[tree]

                @pl.when(jnp.logical_and(chunk >= 0, chunk < TILES))
                def _():
                    start = pl.multiple_of(tile_of(chunk) * TILE + ITEM * tree, ITEM)
                    item = rows.at[core, pl.ds(start, ITEM)]

                    @pl.when(jnp.logical_not(seeded))
                    def _():
                        wait_for(item, tree_recv.at[tree, chunk])

                    spread(item, tree, tree_send, tree_recv.at[tree, chunk])

            @pl.when(jnp.logical_and(owner, jnp.logical_and(lax.rem(t, 2) == 0, t < 12)))
            def _():
                count = lax.div(t, 2)
                group = lax.div(count, 2) + 1
                piece = 4 * lax.div(group, 2) + lax.rem(group, 2) + 2 - 2 * lax.rem(count, 2)
                child_piece(piece, TILE, child_recv.at[piece]).start()

            late = t - LAST

            @pl.when(jnp.logical_and(late >= 0, jnp.logical_not(fed)))
            def _():
                start = pl.multiple_of(tile_of(late) * TILE, TILE)
                item = rows.at[core, pl.ds(start, TILE)]
                remote(item, item, mate_send, mate_recv, mate).start()

        for way in range(2):
            onward = (up, down)[way]
            hops = ring_hops[way]
            piece = t - ring_start[way]
            near = piece >= LONG_PIECES
            reach = jnp.where(near, NEAR_HOPS[way], NZ - 1)

            @pl.when(
                jnp.logical_and(
                    hops <= reach, jnp.logical_and(piece >= 0, piece < RING_PIECES)
                )
            )
            def _():
                rest = piece - LONG_PIECES
                tile = jnp.where(near, 6 + lax.div(rest, 4), lax.div(piece, 2))
                line = jnp.where(near, ITEM * lax.rem(rest, 4), PAIR * way + ITEM * lax.rem(piece, 2))
                which = lax.div(tile, 4)
                place = pl.multiple_of(lax.rem(tile, 4) * TILE + line, ITEM)
                item = cross.at[which, pl.ds(place, ITEM)]

                def pass_on(held, mine):
                    @pl.when(hops < reach)
                    def _():
                        remote(
                            held,
                            item,
                            ring_send.at[way, near.astype(jnp.int32)],
                            ring_recv.at[way, piece],
                            onward,
                        ).start()

                    @pl.when(jnp.logical_and(mine, which != core))
                    def _():
                        remote(
                            held, cross.at[2, pl.ds(place, ITEM)], cross_send, cross_recv, mate
                        ).start()

                @pl.when(hops == 0)
                def _():
                    start = pl.multiple_of((8 * which + 4 * half) * TILE + place, ITEM)
                    mine = piece < (RING_PIECES if way == 0 else LONG_PIECES)

                    @pl.when(mine)
                    def _():
                        cross[which, pl.ds(place, ITEM)] = rows[core, pl.ds(start, ITEM)]

                    pass_on(rows.at[core, pl.ds(start, ITEM)], mine)

                @pl.when(hops > 0)
                def _():
                    wait_for(item, ring_recv.at[way, piece])
                    pass_on(item, True)

        @pl.when(seeded)
        def _():
            for way in range(2):
                onward = (up, down)[way]
                hops = wide_hops[way]
                late = t - SLACK * hops
                chunk = lax.div(late, 2)

                @pl.when(jnp.logical_and(late >= 0, jnp.logical_and(lax.rem(late, 2) == 0, chunk < 4)))
                def _():
                    place = pl.multiple_of(chunk * TILE + PAIR * way, PAIR)
                    item = wide.at[pl.ds(place, PAIR)]

                    @pl.when(hops == 0)
                    def _():
                        wide[pl.ds(place, PAIR)] = rows[0, pl.ds(4 * TILE + place, PAIR)]

                    @pl.when(hops > 0)
                    def _():
                        wait_for(item, climb_recv.at[way, chunk])

                    @pl.when(hops < NZ - 1)
                    def _():
                        remote(
                            item, item, climb_send.at[way], climb_recv.at[way, chunk], onward
                        ).start()

        @pl.when(jnp.logical_and(core == 0, t >= WIDE_STEP))
        def _():
            for tree in range(TREES):
                part = t - WIDE_STEP - depth[tree]

                @pl.when(jnp.logical_and(part >= 0, part < 4))
                def _():
                    place = pl.multiple_of(part * TILE + ITEM * tree, ITEM)
                    item = wide.at[pl.ds(place, ITEM)]

                    @pl.when(jnp.logical_not(seeded))
                    def _():
                        wait_for(item, wide_recv.at[tree, part])

                    spread(item, tree, wide_send, wide_recv.at[tree, part])

            late = t - WIDE_STEP - LAST

            @pl.when(jnp.logical_and(late >= 0, late < 4))
            def _():
                item = wide.at[pl.ds(pl.multiple_of(late * TILE, TILE), TILE)]
                remote(item, item, widemate_send, widemate_recv, mate).start()

        return carry

    lax.fori_loop(0, STEPS, step, 0)

    @pl.when(jnp.logical_not(feeder))
    def _():
        wait_for(rows.at[1 - core], mate_recv)

    wait_for(cross.at[2], cross_recv)

    @pl.when(core == 1)
    def _():
        wait_for(wide, widemate_recv)

    @pl.when(jnp.logical_not(owner))
    def _():
        wait_for(got, child_recv.at[0])

    f0c_t = cross[jnp.where(core == 0, 0, 2)].T
    g1c_t = cross[jnp.where(core == 0, 2, 1)].T
    mixed_t = dot3(inv[1].T, stacked(wide[...]))
    mixed = mixed_t.T
    second = block == 1
    f1c_t = g1c_t - dot3(mixed_t, stacked(f0c_t))
    y0_t = jnp.where(second, mixed, f0c_t - dot3(mixed, stacked(f1c_t)))
    y1_t = jnp.where(second, 0.0, f1c_t)
    for index, value in ((0, y0_t), (1, y1_t), (2, f0c_t)):
        y3[index] = stacked(value)

    def update(step, carry):
        big = pl.ds(pl.multiple_of(step * BIG, BIG), BIG)
        first = jnp.where(z * ROWS + step * BIG < 2 * PW, 2, 0)
        out[big] = dot3(rows[0, big], y3[first]) + dot3(rows[1, big], y3[1])
        for part in range(BIG // TILE):
            tile = step * (BIG // TILE) + part
            lines = pl.ds(pl.multiple_of(tile * TILE, TILE), TILE)
            place = z * TILES + tile
            base = assemble(tile)
            base = jnp.where(jnp.logical_and(block == 0, place >= 4), rows[0, lines], base)
            base = jnp.where(jnp.logical_and(second, place >= 8), rows[1, lines], base)
            out[lines] = base - out[lines]
        pltpu.make_async_copy(out.at[big], out_hbm.at[big], store_sem).start()
        return carry

    lax.fori_loop(0, ROWS // BIG, update, 0)

    wait_for(out, store_sem)
    wait_for(got, child_send)

    @pl.when(feeder)
    def _():
        wait_for(rows.at[0], feed_send)

    @pl.when(jnp.logical_not(fed))
    def _():
        wait_for(rows.at[0], mate_send)

    wait_for(cross.at[0], cross_send)
    for tree in range(TREES):
        for link in range(4):

            @pl.when(forward[tree][link])
            def _():
                wait_for(rows.at[0, pl.ds(0, TILES * ITEM)], tree_send.at[tree, link])

                @pl.when(core == 0)
                def _():
                    wait_for(rows.at[0, pl.ds(0, 4 * ITEM)], wide_send.at[tree, link])

    for way in range(2):

        @pl.when(ring_hops[way] < NZ - 1)
        def _():
            wait_for(rows.at[0, pl.ds(0, LONG_PIECES * ITEM)], ring_send.at[way, 0])

        @pl.when(ring_hops[way] < NEAR_HOPS[way])
        def _():
            wait_for(rows.at[0, pl.ds(0, (RING_PIECES - LONG_PIECES) * ITEM)], ring_send.at[way, 1])

        @pl.when(jnp.logical_and(seeded, wide_hops[way] < NZ - 1))
        def _():
            wait_for(rows.at[0, pl.ds(0, 4 * PAIR)], climb_send.at[way])

    @pl.when(core == 0)
    def _():
        wait_for(wide, widemate_send)


def local(front, children, child_map, inverses):
    hbm = pl.BlockSpec(memory_space=pl.ANY)
    dma = pltpu.SemaphoreType.DMA
    return pl.pallas_call(
        kernel,
        out_shape=jax.ShapeDtypeStruct((ROWS, COLS), F32),
        in_specs=[pl.BlockSpec(memory_space=pltpu.SMEM), hbm, hbm, hbm],
        out_specs=hbm,
        scratch_shapes=[
            pltpu.VMEM((ROWS, COLS), F32),
            pltpu.VMEM((CHILD_ROWS, HALF_COLS), F32),
            pltpu.VMEM((CHILD_ROWS, HALF_COLS), F32),
            pltpu.VMEM((2, PW, PW), F32),
            pltpu.VMEM((2, 3 * PW, PW), BF16),
            pltpu.VMEM((2, ROWS, PW), F32),
            pltpu.VMEM((3, PW, PW), F32),
            pltpu.VMEM((PW, PW), F32),
            pltpu.VMEM((3, 3 * PW, COLS), BF16),
            pltpu.VMEM((ROWS, COLS), F32),
            dma((3,)),
            dma,
            dma,
            dma((8,)),
            dma((TREES, 4)),
            dma((TREES, TILES)),
            dma,
            dma,
            dma,
            dma((2, 2)),
            dma((2, RING_PIECES)),
            dma,
            dma,
            dma((2,)),
            dma((2, 4)),
            dma((TREES, 4)),
            dma((TREES, 4)),
            dma,
            dma,
        ],
        compiler_params=pltpu.CompilerParams(
            collective_id=0, has_side_effects=True, vmem_limit_bytes=56 * 1024 * 1024
        ),
    )(child_map, front, children, inverses)


def solution(mesh):
    return jax.shard_map(
        local,
        mesh=mesh,
        in_specs=(P("row", ("col", "half")), P("half", "row", "col"), P(), P()),
        out_specs=P("row", ("col", "half")),
        check_vma=False,
    )
```

```python
import jax
import jax.numpy as jnp
from jax import lax
from jax.experimental import pallas as pl
from jax.experimental.pallas import tpu as pltpu
from jax.sharding import PartitionSpec as P

TILE = 128
PW = 512
ROWS = 2048
COLS = 512
CHILD_ROWS = 1024
HALF_COLS = 256
TILES = ROWS // TILE
BIG = 256
ITEM = 32
PAIR = 2 * ITEM
TREES = 4
NZ = 8
RING_PIECES = 20
LONG_PIECES = 12
NEAR_HOPS = (4, 3)
SLACK = 3
CHILD_STEP = 17
CHILD_PIECES = 32
EARLY = 8
LAST = 5 * SLACK
WIDE_STEP = 3 + 7 * SLACK
STEPS = LAST + LONG_PIECES + 1 + 7 * SLACK
F32 = jnp.float32
BF16 = jnp.bfloat16


def split(value):
    high = value.astype(BF16)
    return high, (value - high.astype(F32)).astype(BF16)


def dot(left, right):
    return lax.dot_general(left, right, (((1,), (0,)), ((), ())), preferred_element_type=F32)


def stacked(value):
    high, low = split(value)
    return jnp.concatenate([high, low, high], axis=0)


def dot3(left, right):
    high, low = split(left)
    return dot(jnp.concatenate([high, high, low], axis=1), right)


def tile_of(chunk):
    return 8 * lax.div(chunk, 8) + 4 - 4 * lax.rem(chunk, 2) + lax.div(lax.rem(chunk, 8), 2)


def kernel(
    map_ref,
    front_hbm,
    child_hbm,
    inv_hbm,
    out_hbm,
    front,
    own,
    got,
    inv,
    inv3,
    rows,
    cross,
    wide,
    y3,
    out,
    load_sem,
    store_sem,
    child_send,
    child_recv,
    tree_send,
    tree_recv,
    feed_send,
    mate_send,
    mate_recv,
    ring_send,
    ring_recv,
    cross_send,
    cross_recv,
    climb_send,
    climb_recv,
    wide_send,
    wide_recv,
    widemate_send,
    widemate_recv,
):
    half = lax.axis_index("half")
    z = lax.axis_index("row")
    col = lax.axis_index("col")
    core = col % 2
    x = (col // 2) % 4
    yh = col // 8
    y = 2 * yh + half
    block = 2 * col + half

    mate = {"col": col + 1 - 2 * core}
    other = {"half": 1 - half}
    near_x = {"col": col + 2 * (1 - 2 * (x % 2))}
    far_x = {"col": col + 2 * (3 - 2 * x)}
    far_y = {"half": 1 - half, "col": col + 8 * (1 - 2 * yh)}
    links = (other, near_x, far_y, far_x)
    up = {"row": (z + 1) % NZ}
    down = {"row": (z + NZ - 1) % NZ}

    def remote(src, dst, send, recv, peer):
        return pltpu.make_async_remote_copy(
            src_ref=src,
            dst_ref=dst,
            send_sem=send,
            recv_sem=recv,
            device_id=peer,
            device_id_type=pl.DeviceIdType.MESH,
        )

    def wait_for(ref, sem):
        pltpu.make_async_copy(ref, ref, sem).wait()

    bits = (((y + 1) // 2 + core) % 2, ((x + 1) // 2) % 2, yh, x // 2)
    root = (bits[0] + bits[1] + bits[2] + bits[3]) == 0
    depth = []
    forward = []
    for tree in range(TREES):
        turned = [bits[(tree + 1 + k) % 4] for k in range(4)]
        turned[3] = 1 - turned[3]
        weight = turned[0] + turned[1] + turned[2] + turned[3]
        depth.append(jnp.where(root, 0, SLACK * (1 + weight)))
        flags = [None] * 4 + [jnp.logical_or(root, turned[3] == 0)]
        for k in range(4):
            above = turned[k]
            for later in range(k + 1, 4):
                above = above + turned[later]
            flag = jnp.logical_and(jnp.logical_not(root), above == 0)
            if k == 3:
                flag = jnp.logical_or(root, jnp.logical_and(flag, weight > 0))
            flags[(tree + 1 + k) % 4] = flag
        forward.append(flags)

    owner = jnp.logical_and(jnp.logical_and(x == 0, core == 0), y < 2)
    feeder = jnp.logical_and(owner, half == 1)
    fed = jnp.logical_and(root, core == 1)
    seeded = jnp.logical_and(root, core == 0)

    source = 4 * yh + x
    ring_hops = [(z - source + NZ) % NZ, (source - z + NZ) % NZ]
    wide_hops = [z, (NZ - z) % NZ]
    deepest = jnp.maximum(jnp.maximum(depth[0], depth[1]), jnp.maximum(depth[2], depth[3]))
    ring_start = [1 - half + deepest + SLACK * hops for hops in ring_hops]

    loads = [
        pltpu.make_async_copy(front_hbm, front, load_sem.at[0]),
        pltpu.make_async_copy(
            child_hbm.at[0, :, pl.ds(pl.multiple_of(half * HALF_COLS, HALF_COLS), HALF_COLS)],
            own,
            load_sem.at[1],
        ),
        pltpu.make_async_copy(inv_hbm, inv, load_sem.at[2]),
    ]
    for load in loads:
        load.start()
    barrier = pltpu.get_barrier_semaphore()
    for peer in (mate, up, down) + links:
        pl.semaphore_signal(barrier, inc=1, device_id=peer, device_id_type=pl.DeviceIdType.MESH)
    pl.semaphore_wait(barrier, 7)

    def child_piece(piece, count, recv):
        theirs = pl.ds(pl.multiple_of((1 - half) * HALF_COLS, HALF_COLS), HALF_COLS)
        lines = pl.ds(pl.multiple_of(piece * count, count), count)
        return remote(
            child_hbm.at[0, lines, theirs], got.at[lines], child_send, recv, other
        )

    @pl.when(owner)
    def _():
        for piece in (2, 0):
            child_piece(piece, TILE, child_recv.at[piece]).start()

    early = x > 0

    @pl.when(early)
    def _():
        child_piece(0, EARLY * (CHILD_ROWS // CHILD_PIECES), child_recv.at[0]).start()

    for load in loads:
        load.wait()

    @pl.when(owner)
    def _():
        inv3[...] = stacked(inv[half])

    def assemble(tile):
        pair = lax.div(tile, 2)
        lines = pl.ds(pl.multiple_of(tile * TILE, TILE), TILE)
        child_lines = pl.ds(pl.multiple_of(pair * TILE, TILE), TILE)
        row_tile = z * (TILES // 2) + pair
        parts = []
        for q in range(4):
            value = front[lines, pl.ds(q * TILE, TILE)]
            col_tile = 4 * col + 2 * half + q // 2
            for ref, which in ((own, half), (got, 1 - half)):
                row_bit = map_ref[which, row_tile] - 2 * row_tile
                col_bit = map_ref[which, col_tile] - 2 * col_tile
                hit = jnp.logical_and(row_bit == lax.rem(tile, 2), col_bit == q % 2)
                value = value + jnp.where(hit, ref[child_lines, pl.ds(q // 2 * TILE, TILE)], 0.0)
            parts.append(value)
        return jnp.concatenate(parts, axis=1)

    def spread(item, tree, send, recv):
        def give(link):
            @pl.when(forward[tree][link])
            def _():
                remote(item, item, send.at[tree, link], recv, links[link]).start()

        @pl.when(forward[tree][4])
        def _():
            give(tree)
            give((tree + 3) % 4)

            @pl.when(forward[tree][(tree + 2) % 4])
            def _():
                give((tree + 2) % 4)
                give((tree + 1) % 4)

    def step(t, carry):
        @pl.when(jnp.logical_and(owner, t < TILES))
        def _():
            tile = tile_of(t)

            @pl.when(lax.rem(t, 4) < 2)
            def _():
                piece = lax.div(tile, 2)
                wait_for(got.at[pl.ds(pl.multiple_of(piece * TILE, TILE), TILE)], child_recv.at[piece])

            slab = assemble(tile)
            factor = dot3(slab, inv3[...])
            keep = z * TILES + tile >= 4 * (half + 1)
            start = pl.multiple_of(tile * TILE, TILE)
            rows[half, pl.ds(start, TILE)] = jnp.where(keep, factor, 0.0)

            @pl.when(feeder)
            def _():
                for tree in range(TREES):
                    item = rows.at[1, pl.ds(start + ITEM * tree, ITEM)]
                    remote(item, item, feed_send, tree_recv.at[tree, t], mate).start()

        @pl.when(
            jnp.logical_and(
                jnp.logical_not(owner),
                jnp.logical_and(
                    t >= CHILD_STEP + jnp.where(early, EARLY, 0), t < CHILD_STEP + CHILD_PIECES
                ),
            )
        )
        def _():
            child_piece(t - CHILD_STEP, CHILD_ROWS // CHILD_PIECES, child_recv.at[0]).start()

        @pl.when(t < TILES + LAST)
        def _():
            for tree in range(TREES):
                chunk = t - depth[tree]

                @pl.when(jnp.logical_and(chunk >= 0, chunk < TILES))
                def _():
                    start = pl.multiple_of(tile_of(chunk) * TILE + ITEM * tree, ITEM)
                    item = rows.at[core, pl.ds(start, ITEM)]

                    @pl.when(jnp.logical_not(seeded))
                    def _():
                        wait_for(item, tree_recv.at[tree, chunk])

                    spread(item, tree, tree_send, tree_recv.at[tree, chunk])

            @pl.when(jnp.logical_and(owner, jnp.logical_and(lax.rem(t, 2) == 0, t < 12)))
            def _():
                count = lax.div(t, 2)
                group = lax.div(count, 2) + 1
                piece = 4 * lax.div(group, 2) + lax.rem(group, 2) + 2 - 2 * lax.rem(count, 2)
                child_piece(piece, TILE, child_recv.at[piece]).start()

            late = t - LAST

            @pl.when(jnp.logical_and(late >= 0, jnp.logical_not(fed)))
            def _():
                start = pl.multiple_of(tile_of(late) * TILE, TILE)
                item = rows.at[core, pl.ds(start, TILE)]
                remote(item, item, mate_send, mate_recv, mate).start()

        for way in range(2):
            onward = (up, down)[way]
            hops = ring_hops[way]
            piece = t - ring_start[way]
            near = piece >= LONG_PIECES
            reach = jnp.where(near, NEAR_HOPS[way], NZ - 1)

            @pl.when(
                jnp.logical_and(
                    hops <= reach, jnp.logical_and(piece >= 0, piece < RING_PIECES)
                )
            )
            def _():
                rest = piece - LONG_PIECES
                tile = jnp.where(near, 6 + lax.div(rest, 4), lax.div(piece, 2))
                line = jnp.where(near, ITEM * lax.rem(rest, 4), PAIR * way + ITEM * lax.rem(piece, 2))
                which = lax.div(tile, 4)
                place = pl.multiple_of(lax.rem(tile, 4) * TILE + line, ITEM)
                item = cross.at[which, pl.ds(place, ITEM)]

                def pass_on(held, mine):
                    @pl.when(hops < reach)
                    def _():
                        remote(
                            held,
                            item,
                            ring_send.at[way, near.astype(jnp.int32)],
                            ring_recv.at[way, piece],
                            onward,
                        ).start()

                    @pl.when(jnp.logical_and(mine, which != core))
                    def _():
                        remote(
                            held, cross.at[2, pl.ds(place, ITEM)], cross_send, cross_recv, mate
                        ).start()

                @pl.when(hops == 0)
                def _():
                    start = pl.multiple_of((8 * which + 4 * half) * TILE + place, ITEM)
                    mine = piece < (RING_PIECES if way == 0 else LONG_PIECES)

                    @pl.when(mine)
                    def _():
                        cross[which, pl.ds(place, ITEM)] = rows[core, pl.ds(start, ITEM)]

                    pass_on(rows.at[core, pl.ds(start, ITEM)], mine)

                @pl.when(hops > 0)
                def _():
                    wait_for(item, ring_recv.at[way, piece])
                    pass_on(item, True)

        @pl.when(seeded)
        def _():
            for way in range(2):
                onward = (up, down)[way]
                hops = wide_hops[way]
                late = t - SLACK * hops
                chunk = lax.div(late, 2)

                @pl.when(jnp.logical_and(late >= 0, jnp.logical_and(lax.rem(late, 2) == 0, chunk < 4)))
                def _():
                    place = pl.multiple_of(chunk * TILE + PAIR * way, PAIR)
                    item = wide.at[pl.ds(place, PAIR)]

                    @pl.when(hops == 0)
                    def _():
                        wide[pl.ds(place, PAIR)] = rows[0, pl.ds(4 * TILE + place, PAIR)]

                    @pl.when(hops > 0)
                    def _():
                        wait_for(item, climb_recv.at[way, chunk])

                    @pl.when(hops < NZ - 1)
                    def _():
                        remote(
                            item, item, climb_send.at[way], climb_recv.at[way, chunk], onward
                        ).start()

        @pl.when(jnp.logical_and(core == 0, t >= WIDE_STEP))
        def _():
            for tree in range(TREES):
                part = t - WIDE_STEP - depth[tree]

                @pl.when(jnp.logical_and(part >= 0, part < 4))
                def _():
                    place = pl.multiple_of(part * TILE + ITEM * tree, ITEM)
                    item = wide.at[pl.ds(place, ITEM)]

                    @pl.when(jnp.logical_not(seeded))
                    def _():
                        wait_for(item, wide_recv.at[tree, part])

                    spread(item, tree, wide_send, wide_recv.at[tree, part])

            late = t - WIDE_STEP - LAST

            @pl.when(jnp.logical_and(late >= 0, late < 4))
            def _():
                item = wide.at[pl.ds(pl.multiple_of(late * TILE, TILE), TILE)]
                remote(item, item, widemate_send, widemate_recv, mate).start()

        return carry

    lax.fori_loop(0, STEPS, step, 0)

    @pl.when(jnp.logical_not(feeder))
    def _():
        wait_for(rows.at[1 - core], mate_recv)

    wait_for(cross.at[2], cross_recv)

    @pl.when(core == 1)
    def _():
        wait_for(wide, widemate_recv)

    @pl.when(jnp.logical_not(owner))
    def _():
        wait_for(got, child_recv.at[0])

    f0c_t = cross[jnp.where(core == 0, 0, 2)].T
    g1c_t = cross[jnp.where(core == 0, 2, 1)].T
    mixed_t = dot3(inv[1].T, stacked(wide[...]))
    mixed = mixed_t.T
    second = block == 1
    f1c_t = g1c_t - dot3(mixed_t, stacked(f0c_t))
    y0_t = jnp.where(second, mixed, f0c_t - dot3(mixed, stacked(f1c_t)))
    y1_t = jnp.where(second, 0.0, f1c_t)
    for index, value in ((0, y0_t), (1, y1_t), (2, f0c_t)):
        y3[index] = stacked(value)

    def update(step, carry):
        big = pl.ds(pl.multiple_of(step * BIG, BIG), BIG)
        first = jnp.where(z * ROWS + step * BIG < 2 * PW, 2, 0)
        out[big] = dot3(rows[0, big], y3[first]) + dot3(rows[1, big], y3[1])
        for part in range(BIG // TILE):
            tile = step * (BIG // TILE) + part
            lines = pl.ds(pl.multiple_of(tile * TILE, TILE), TILE)
            place = z * TILES + tile
            base = assemble(tile)
            base = jnp.where(jnp.logical_and(block == 0, place >= 4), rows[0, lines], base)
            base = jnp.where(jnp.logical_and(second, place >= 8), rows[1, lines], base)
            out[lines] = base - out[lines]
        pltpu.make_async_copy(out.at[big], out_hbm.at[big], store_sem).start()
        return carry

    lax.fori_loop(0, ROWS // BIG, update, 0)

    wait_for(out, store_sem)
    wait_for(got, child_send)

    @pl.when(feeder)
    def _():
        wait_for(rows.at[0], feed_send)

    @pl.when(jnp.logical_not(fed))
    def _():
        wait_for(rows.at[0], mate_send)

    wait_for(cross.at[0], cross_send)
    for tree in range(TREES):
        for link in range(4):

            @pl.when(forward[tree][link])
            def _():
                wait_for(rows.at[0, pl.ds(0, TILES * ITEM)], tree_send.at[tree, link])

                @pl.when(core == 0)
                def _():
                    wait_for(rows.at[0, pl.ds(0, 4 * ITEM)], wide_send.at[tree, link])

    for way in range(2):

        @pl.when(ring_hops[way] < NZ - 1)
        def _():
            wait_for(rows.at[0, pl.ds(0, LONG_PIECES * ITEM)], ring_send.at[way, 0])

        @pl.when(ring_hops[way] < NEAR_HOPS[way])
        def _():
            wait_for(rows.at[0, pl.ds(0, (RING_PIECES - LONG_PIECES) * ITEM)], ring_send.at[way, 1])

        @pl.when(jnp.logical_and(seeded, wide_hops[way] < NZ - 1))
        def _():
            wait_for(rows.at[0, pl.ds(0, 4 * PAIR)], climb_send.at[way])

    @pl.when(core == 0)
    def _():
        wait_for(wide, widemate_send)


def local(front, children, child_map, inverses):
    hbm = pl.BlockSpec(memory_space=pl.ANY)
    dma = pltpu.SemaphoreType.DMA
    return pl.pallas_call(
        kernel,
        out_shape=jax.ShapeDtypeStruct((ROWS, COLS), F32),
        in_specs=[pl.BlockSpec(memory_space=pltpu.SMEM), hbm, hbm, hbm],
        out_specs=hbm,
        scratch_shapes=[
            pltpu.VMEM((ROWS, COLS), F32),
            pltpu.VMEM((CHILD_ROWS, HALF_COLS), F32),
            pltpu.VMEM((CHILD_ROWS, HALF_COLS), F32),
            pltpu.VMEM((2, PW, PW), F32),
            pltpu.VMEM((3 * PW, PW), BF16),
            pltpu.VMEM((2, ROWS, PW), F32),
            pltpu.VMEM((3, PW, PW), F32),
            pltpu.VMEM((PW, PW), F32),
            pltpu.VMEM((3, 3 * PW, COLS), BF16),
            pltpu.VMEM((ROWS, COLS), F32),
            dma((3,)),
            dma,
            dma,
            dma((8,)),
            dma((TREES, 4)),
            dma((TREES, TILES)),
            dma,
            dma,
            dma,
            dma((2, 2)),
            dma((2, RING_PIECES)),
            dma,
            dma,
            dma((2,)),
            dma((2, 4)),
            dma((TREES, 4)),
            dma((TREES, 4)),
            dma,
            dma,
        ],
        compiler_params=pltpu.CompilerParams(
            collective_id=0, has_side_effects=True, vmem_limit_bytes=56 * 1024 * 1024
        ),
    )(child_map, front, children, inverses)


def solution(mesh):
    return jax.shard_map(
        local,
        mesh=mesh,
        in_specs=(P("row", ("col", "half")), P("half", "row", "col"), P(), P()),
        out_specs=P("row", ("col", "half")),
        check_vma=False,
    )
```

```python
import jax
import jax.numpy as jnp
from jax import lax
from jax.experimental import pallas as pl
from jax.experimental.pallas import tpu as pltpu
from jax.sharding import PartitionSpec as P

TILE = 128
PW = 512
ROWS = 2048
COLS = 512
CHILD_ROWS = 1024
HALF_COLS = 256
TILES = ROWS // TILE
BIG = 256
ITEM = 32
PAIR = 2 * ITEM
TREES = 4
NZ = 8
RING_PIECES = 20
LONG_PIECES = 12
NEAR_HOPS = (4, 3)
SLACK = 3
CHILD_STEP = 14
CHILD_PIECES = 32
EARLY = 12
LAST = 5 * SLACK
WIDE_STEP = 3 + 7 * SLACK
STEPS = LAST + LONG_PIECES + 1 + 7 * SLACK
F32 = jnp.float32
BF16 = jnp.bfloat16


def split(value):
    high = value.astype(BF16)
    return high, (value - high.astype(F32)).astype(BF16)


def dot(left, right):
    return lax.dot_general(left, right, (((1,), (0,)), ((), ())), preferred_element_type=F32)


def stacked(value):
    high, low = split(value)
    return jnp.concatenate([high, low, high], axis=0)


def dot3(left, right):
    high, low = split(left)
    return dot(jnp.concatenate([high, high, low], axis=1), right)


def tile_of(chunk):
    return 8 * lax.div(chunk, 8) + 4 - 4 * lax.rem(chunk, 2) + lax.div(lax.rem(chunk, 8), 2)


def kernel(
    map_ref,
    front_hbm,
    child_hbm,
    inv_hbm,
    out_hbm,
    front,
    own,
    got,
    inv,
    inv3,
    rows,
    cross,
    wide,
    y3,
    out,
    load_sem,
    store_sem,
    child_send,
    child_recv,
    tree_send,
    tree_recv,
    feed_send,
    mate_send,
    mate_recv,
    ring_send,
    ring_recv,
    cross_send,
    cross_recv,
    climb_send,
    climb_recv,
    wide_send,
    wide_recv,
    widemate_send,
    widemate_recv,
):
    half = lax.axis_index("half")
    z = lax.axis_index("row")
    col = lax.axis_index("col")
    core = col % 2
    x = (col // 2) % 4
    yh = col // 8
    y = 2 * yh + half
    block = 2 * col + half

    mate = {"col": col + 1 - 2 * core}
    other = {"half": 1 - half}
    near_x = {"col": col + 2 * (1 - 2 * (x % 2))}
    far_x = {"col": col + 2 * (3 - 2 * x)}
    far_y = {"half": 1 - half, "col": col + 8 * (1 - 2 * yh)}
    links = (other, near_x, far_y, far_x)
    up = {"row": (z + 1) % NZ}
    down = {"row": (z + NZ - 1) % NZ}

    def remote(src, dst, send, recv, peer):
        return pltpu.make_async_remote_copy(
            src_ref=src,
            dst_ref=dst,
            send_sem=send,
            recv_sem=recv,
            device_id=peer,
            device_id_type=pl.DeviceIdType.MESH,
        )

    def wait_for(ref, sem):
        pltpu.make_async_copy(ref, ref, sem).wait()

    bits = (((y + 1) // 2 + core) % 2, ((x + 1) // 2) % 2, yh, x // 2)
    root = (bits[0] + bits[1] + bits[2] + bits[3]) == 0
    depth = []
    forward = []
    for tree in range(TREES):
        turned = [bits[(tree + 1 + k) % 4] for k in range(4)]
        turned[3] = 1 - turned[3]
        weight = turned[0] + turned[1] + turned[2] + turned[3]
        depth.append(jnp.where(root, 0, SLACK * (1 + weight)))
        flags = [None] * 4 + [jnp.logical_or(root, turned[3] == 0)]
        for k in range(4):
            above = turned[k]
            for later in range(k + 1, 4):
                above = above + turned[later]
            flag = jnp.logical_and(jnp.logical_not(root), above == 0)
            if k == 3:
                flag = jnp.logical_or(root, jnp.logical_and(flag, weight > 0))
            flags[(tree + 1 + k) % 4] = flag
        forward.append(flags)

    owner = jnp.logical_and(jnp.logical_and(x == 0, core == 0), y < 2)
    feeder = jnp.logical_and(owner, half == 1)
    fed = jnp.logical_and(root, core == 1)
    seeded = jnp.logical_and(root, core == 0)

    source = 4 * yh + x
    ring_hops = [(z - source + NZ) % NZ, (source - z + NZ) % NZ]
    wide_hops = [z, (NZ - z) % NZ]
    deepest = jnp.maximum(jnp.maximum(depth[0], depth[1]), jnp.maximum(depth[2], depth[3]))
    ring_start = [1 - half + deepest + SLACK * hops for hops in ring_hops]

    loads = [
        pltpu.make_async_copy(front_hbm, front, load_sem.at[0]),
        pltpu.make_async_copy(
            child_hbm.at[0, :, pl.ds(pl.multiple_of(half * HALF_COLS, HALF_COLS), HALF_COLS)],
            own,
            load_sem.at[1],
        ),
        pltpu.make_async_copy(inv_hbm, inv, load_sem.at[2]),
    ]
    for load in loads:
        load.start()
    barrier = pltpu.get_barrier_semaphore()
    for peer in (mate, up, down) + links:
        pl.semaphore_signal(barrier, inc=1, device_id=peer, device_id_type=pl.DeviceIdType.MESH)
    pl.semaphore_wait(barrier, 7)

    def child_piece(piece, count, recv):
        theirs = pl.ds(pl.multiple_of((1 - half) * HALF_COLS, HALF_COLS), HALF_COLS)
        lines = pl.ds(pl.multiple_of(piece * count, count), count)
        return remote(
            child_hbm.at[0, lines, theirs], got.at[lines], child_send, recv, other
        )

    @pl.when(owner)
    def _():
        for piece in (2, 0):
            child_piece(piece, TILE, child_recv.at[piece]).start()

    early = jnp.logical_or(x > 0, y > 1)
    child_step = jnp.where(early, CHILD_STEP - 4, CHILD_STEP)

    @pl.when(early)
    def _():
        child_piece(0, EARLY * (CHILD_ROWS // CHILD_PIECES), child_recv.at[0]).start()

    for load in loads:
        load.wait()

    @pl.when(owner)
    def _():
        inv3[...] = stacked(inv[half])

    def assemble(tile):
        pair = lax.div(tile, 2)
        lines = pl.ds(pl.multiple_of(tile * TILE, TILE), TILE)
        child_lines = pl.ds(pl.multiple_of(pair * TILE, TILE), TILE)
        row_tile = z * (TILES // 2) + pair
        parts = []
        for q in range(4):
            value = front[lines, pl.ds(q * TILE, TILE)]
            col_tile = 4 * col + 2 * half + q // 2
            for ref, which in ((own, half), (got, 1 - half)):
                row_bit = map_ref[which, row_tile] - 2 * row_tile
                col_bit = map_ref[which, col_tile] - 2 * col_tile
                hit = jnp.logical_and(row_bit == lax.rem(tile, 2), col_bit == q % 2)
                value = value + jnp.where(hit, ref[child_lines, pl.ds(q // 2 * TILE, TILE)], 0.0)
            parts.append(value)
        return jnp.concatenate(parts, axis=1)

    def spread(item, tree, send, recv):
        def give(link):
            @pl.when(forward[tree][link])
            def _():
                remote(item, item, send.at[tree, link], recv, links[link]).start()

        @pl.when(forward[tree][4])
        def _():
            give(tree)
            give((tree + 3) % 4)

            @pl.when(forward[tree][(tree + 2) % 4])
            def _():
                give((tree + 2) % 4)
                give((tree + 1) % 4)

    def step(t, carry):
        @pl.when(jnp.logical_and(owner, t < TILES))
        def _():
            tile = tile_of(t)

            @pl.when(lax.rem(t, 4) < 2)
            def _():
                piece = lax.div(tile, 2)
                wait_for(got.at[pl.ds(pl.multiple_of(piece * TILE, TILE), TILE)], child_recv.at[piece])

            slab = assemble(tile)
            factor = dot3(slab, inv3[...])
            keep = z * TILES + tile >= 4 * (half + 1)
            start = pl.multiple_of(tile * TILE, TILE)
            rows[half, pl.ds(start, TILE)] = jnp.where(keep, factor, 0.0)

            @pl.when(feeder)
            def _():
                for tree in range(TREES):
                    item = rows.at[1, pl.ds(start + ITEM * tree, ITEM)]
                    remote(item, item, feed_send, tree_recv.at[tree, t], mate).start()

        @pl.when(
            jnp.logical_and(
                jnp.logical_not(owner),
                jnp.logical_and(
                    t >= child_step + jnp.where(early, EARLY, 0), t < child_step + CHILD_PIECES
                ),
            )
        )
        def _():
            child_piece(t - child_step, CHILD_ROWS // CHILD_PIECES, child_recv.at[0]).start()

        @pl.when(t < TILES + LAST)
        def _():
            for tree in range(TREES):
                chunk = t - depth[tree]

                @pl.when(jnp.logical_and(chunk >= 0, chunk < TILES))
                def _():
                    start = pl.multiple_of(tile_of(chunk) * TILE + ITEM * tree, ITEM)
                    item = rows.at[core, pl.ds(start, ITEM)]

                    @pl.when(jnp.logical_not(seeded))
                    def _():
                        wait_for(item, tree_recv.at[tree, chunk])

                    spread(item, tree, tree_send, tree_recv.at[tree, chunk])

            @pl.when(jnp.logical_and(owner, jnp.logical_and(lax.rem(t, 2) == 0, t < 12)))
            def _():
                count = lax.div(t, 2)
                group = lax.div(count, 2) + 1
                piece = 4 * lax.div(group, 2) + lax.rem(group, 2) + 2 - 2 * lax.rem(count, 2)
                child_piece(piece, TILE, child_recv.at[piece]).start()

            late = t - LAST

            @pl.when(jnp.logical_and(late >= 0, jnp.logical_not(fed)))
            def _():
                start = pl.multiple_of(tile_of(late) * TILE, TILE)
                item = rows.at[core, pl.ds(start, TILE)]
                remote(item, item, mate_send, mate_recv, mate).start()

        for way in range(2):
            onward = (up, down)[way]
            hops = ring_hops[way]
            piece = t - ring_start[way]
            near = piece >= LONG_PIECES
            reach = jnp.where(near, NEAR_HOPS[way], NZ - 1)

            @pl.when(
                jnp.logical_and(
                    hops <= reach, jnp.logical_and(piece >= 0, piece < RING_PIECES)
                )
            )
            def _():
                rest = piece - LONG_PIECES
                tile = jnp.where(near, 6 + lax.div(rest, 4), lax.div(piece, 2))
                line = jnp.where(near, ITEM * lax.rem(rest, 4), PAIR * way + ITEM * lax.rem(piece, 2))
                which = lax.div(tile, 4)
                place = pl.multiple_of(lax.rem(tile, 4) * TILE + line, ITEM)
                item = cross.at[which, pl.ds(place, ITEM)]

                def pass_on(held, mine):
                    @pl.when(hops < reach)
                    def _():
                        remote(
                            held,
                            item,
                            ring_send.at[way, near.astype(jnp.int32)],
                            ring_recv.at[way, piece],
                            onward,
                        ).start()

                    @pl.when(jnp.logical_and(mine, which != core))
                    def _():
                        remote(
                            held, cross.at[2, pl.ds(place, ITEM)], cross_send, cross_recv, mate
                        ).start()

                @pl.when(hops == 0)
                def _():
                    start = pl.multiple_of((8 * which + 4 * half) * TILE + place, ITEM)
                    mine = piece < (RING_PIECES if way == 0 else LONG_PIECES)

                    @pl.when(mine)
                    def _():
                        cross[which, pl.ds(place, ITEM)] = rows[core, pl.ds(start, ITEM)]

                    pass_on(rows.at[core, pl.ds(start, ITEM)], mine)

                @pl.when(hops > 0)
                def _():
                    wait_for(item, ring_recv.at[way, piece])
                    pass_on(item, True)

        @pl.when(seeded)
        def _():
            for way in range(2):
                onward = (up, down)[way]
                hops = wide_hops[way]
                late = t - SLACK * hops
                chunk = lax.div(late, 2)

                @pl.when(jnp.logical_and(late >= 0, jnp.logical_and(lax.rem(late, 2) == 0, chunk < 4)))
                def _():
                    place = pl.multiple_of(chunk * TILE + PAIR * way, PAIR)
                    item = wide.at[pl.ds(place, PAIR)]

                    @pl.when(hops == 0)
                    def _():
                        wide[pl.ds(place, PAIR)] = rows[0, pl.ds(4 * TILE + place, PAIR)]

                    @pl.when(hops > 0)
                    def _():
                        wait_for(item, climb_recv.at[way, chunk])

                    @pl.when(hops < NZ - 1)
                    def _():
                        remote(
                            item, item, climb_send.at[way], climb_recv.at[way, chunk], onward
                        ).start()

        @pl.when(jnp.logical_and(core == 0, t >= WIDE_STEP))
        def _():
            for tree in range(TREES):
                part = t - WIDE_STEP - depth[tree]

                @pl.when(jnp.logical_and(part >= 0, part < 4))
                def _():
                    place = pl.multiple_of(part * TILE + ITEM * tree, ITEM)
                    item = wide.at[pl.ds(place, ITEM)]

                    @pl.when(jnp.logical_not(seeded))
                    def _():
                        wait_for(item, wide_recv.at[tree, part])

                    spread(item, tree, wide_send, wide_recv.at[tree, part])

            late = t - WIDE_STEP - LAST

            @pl.when(jnp.logical_and(late >= 0, late < 4))
            def _():
                item = wide.at[pl.ds(pl.multiple_of(late * TILE, TILE), TILE)]
                remote(item, item, widemate_send, widemate_recv, mate).start()

        return carry

    lax.fori_loop(0, STEPS, step, 0)

    @pl.when(jnp.logical_not(feeder))
    def _():
        wait_for(rows.at[1 - core], mate_recv)

    wait_for(cross.at[2], cross_recv)

    @pl.when(core == 1)
    def _():
        wait_for(wide, widemate_recv)

    @pl.when(jnp.logical_not(owner))
    def _():
        wait_for(got, child_recv.at[0])

    f0c_t = cross[jnp.where(core == 0, 0, 2)].T
    g1c_t = cross[jnp.where(core == 0, 2, 1)].T
    mixed_t = dot3(inv[1].T, stacked(wide[...]))
    mixed = mixed_t.T
    second = block == 1
    f1c_t = g1c_t - dot3(mixed_t, stacked(f0c_t))
    y0_t = jnp.where(second, mixed, f0c_t - dot3(mixed, stacked(f1c_t)))
    y1_t = jnp.where(second, 0.0, f1c_t)
    for index, value in ((0, y0_t), (1, y1_t), (2, f0c_t)):
        y3[index] = stacked(value)

    def update(step, carry):
        big = pl.ds(pl.multiple_of(step * BIG, BIG), BIG)
        first = jnp.where(z * ROWS + step * BIG < 2 * PW, 2, 0)
        out[big] = dot3(rows[0, big], y3[first]) + dot3(rows[1, big], y3[1])
        for part in range(BIG // TILE):
            tile = step * (BIG // TILE) + part
            lines = pl.ds(pl.multiple_of(tile * TILE, TILE), TILE)
            place = z * TILES + tile
            base = assemble(tile)
            base = jnp.where(jnp.logical_and(block == 0, place >= 4), rows[0, lines], base)
            base = jnp.where(jnp.logical_and(second, place >= 8), rows[1, lines], base)
            out[lines] = base - out[lines]
        pltpu.make_async_copy(out.at[big], out_hbm.at[big], store_sem).start()
        return carry

    lax.fori_loop(0, ROWS // BIG, update, 0)

    wait_for(out, store_sem)
    wait_for(got, child_send)

    @pl.when(feeder)
    def _():
        wait_for(rows.at[0], feed_send)

    @pl.when(jnp.logical_not(fed))
    def _():
        wait_for(rows.at[0], mate_send)

    wait_for(cross.at[0], cross_send)
    for tree in range(TREES):
        for link in range(4):

            @pl.when(forward[tree][link])
            def _():
                wait_for(rows.at[0, pl.ds(0, TILES * ITEM)], tree_send.at[tree, link])

                @pl.when(core == 0)
                def _():
                    wait_for(rows.at[0, pl.ds(0, 4 * ITEM)], wide_send.at[tree, link])

    for way in range(2):

        @pl.when(ring_hops[way] < NZ - 1)
        def _():
            wait_for(rows.at[0, pl.ds(0, LONG_PIECES * ITEM)], ring_send.at[way, 0])

        @pl.when(ring_hops[way] < NEAR_HOPS[way])
        def _():
            wait_for(rows.at[0, pl.ds(0, (RING_PIECES - LONG_PIECES) * ITEM)], ring_send.at[way, 1])

        @pl.when(jnp.logical_and(seeded, wide_hops[way] < NZ - 1))
        def _():
            wait_for(rows.at[0, pl.ds(0, 4 * PAIR)], climb_send.at[way])

    @pl.when(core == 0)
    def _():
        wait_for(wide, widemate_send)


def local(front, children, child_map, inverses):
    hbm = pl.BlockSpec(memory_space=pl.ANY)
    dma = pltpu.SemaphoreType.DMA
    return pl.pallas_call(
        kernel,
        out_shape=jax.ShapeDtypeStruct((ROWS, COLS), F32),
        in_specs=[pl.BlockSpec(memory_space=pltpu.SMEM), hbm, hbm, hbm],
        out_specs=hbm,
        scratch_shapes=[
            pltpu.VMEM((ROWS, COLS), F32),
            pltpu.VMEM((CHILD_ROWS, HALF_COLS), F32),
            pltpu.VMEM((CHILD_ROWS, HALF_COLS), F32),
            pltpu.VMEM((2, PW, PW), F32),
            pltpu.VMEM((3 * PW, PW), BF16),
            pltpu.VMEM((2, ROWS, PW), F32),
            pltpu.VMEM((3, PW, PW), F32),
            pltpu.VMEM((PW, PW), F32),
            pltpu.VMEM((3, 3 * PW, COLS), BF16),
            pltpu.VMEM((ROWS, COLS), F32),
            dma((3,)),
            dma,
            dma,
            dma((8,)),
            dma((TREES, 4)),
            dma((TREES, TILES)),
            dma,
            dma,
            dma,
            dma((2, 2)),
            dma((2, RING_PIECES)),
            dma,
            dma,
            dma((2,)),
            dma((2, 4)),
            dma((TREES, 4)),
            dma((TREES, 4)),
            dma,
            dma,
        ],
        compiler_params=pltpu.CompilerParams(
            collective_id=0, has_side_effects=True, vmem_limit_bytes=56 * 1024 * 1024
        ),
    )(child_map, front, children, inverses)


def solution(mesh):
    return jax.shard_map(
        local,
        mesh=mesh,
        in_specs=(P("row", ("col", "half")), P("half", "row", "col"), P(), P()),
        out_specs=P("row", ("col", "half")),
        check_vma=False,
    )
```
